256 devices in a mesh: ctx: 64 (over x, z, core), head: 4 (over y).
Axes of the slice: x: 4, y: 4, z: 8, core: 2. Of those that a mesh axis runs over, the one named last changes fastest.
Arguments:
- prefix_query: bfloat16 [2048, 8192], P(('ctx', 'head')), may hold values from -7 to 7
- prefix_key: bfloat16 [2048, 1024], P(('ctx', 'head')), may hold values from -6 to 6
- prefix_value: bfloat16 [2048, 1024], P(('ctx', 'head')), may hold values from -6 to 6
- prefix_cotangent: bfloat16 [2048, 8192], P(('ctx', 'head')), may hold values from -6 to 6
- reply_query: bfloat16 [16384, 8192], P('ctx', 'head'), may hold values from -7 to 7
- reply_key: bfloat16 [16384, 1024], P('ctx', 'head'), may hold values from -6 to 6
- reply_value: bfloat16 [16384, 1024], P('ctx', 'head'), may hold values from -6 to 6
- reply_cotangent: bfloat16 [16384, 8192], P('ctx', 'head'), may hold values from -6 to 6
- parent: int32 [64], P('ctx'), may hold values from 0 to 1
- lengths: int32 [64], P('ctx'), may hold values from 1 to 256, 10240 in all
Outputs:
- prefix_output: bfloat16 [2048, 8192], P(('ctx', 'head'))
- prefix_query_gradient: bfloat16 [2048, 8192], P(('ctx', 'head'))
- prefix_key_gradient: bfloat16 [2048, 1024], P(('ctx', 'head'))
- prefix_value_gradient: bfloat16 [2048, 1024], P(('ctx', 'head'))
- reply_output: bfloat16 [16384, 8192], P('ctx', 'head')
- reply_query_gradient: bfloat16 [16384, 8192], P('ctx', 'head')
- reply_key_gradient: bfloat16 [16384, 1024], P('ctx', 'head')
- reply_value_gradient: bfloat16 [16384, 1024], P('ctx', 'head')
The draws below stay inside these ranges and needn't reach their ends.
Inputs may be any that keep to these rules, and one draw needn't show every extreme that they name: The lengths sum to 10240 and the longest is exactly 256.
All inputs are finite; a program needn't handle non-finite values. No bound on the sum of `lengths` on one device may be relied on, other than what follows from the above.
Results may differ from the reference program's by a relative error of at most 0.035.
Values may be sent and summed in bfloat16 or wider, within the bound.
No kernel may reach another device: no remote copies, remote signals or barrier semaphores. Data moves between devices by JAX's collectives and lax.ppermute only.
A program may use at most 128 MiB of HBM per device.

```python
import math
import jax
import jax.numpy as jnp
import numpy as np
from jax import lax

Q_HEADS = 64
KV_HEADS = 8
HD = 128
GROUP = 8
PROMPTS = 2
RESP_MAX = 256
PREFIX_LEN = 1024
PREFIX_ROWS = 2048
RESPONSES = 64


def draw_prefix_query(key, part):
    key = jax.random.fold_in(key, 3)
    drawn = 2.0 * jax.random.normal(key, (PREFIX_ROWS, Q_HEADS * HD), jnp.float32)
    return jnp.clip(drawn, -7.0, 7.0).astype(jnp.bfloat16)


def draw_prefix_key(key, part):
    key = jax.random.fold_in(key, 4)
    drawn = jax.random.normal(key, (PREFIX_ROWS, KV_HEADS * HD), jnp.float32)
    return jnp.clip(drawn, -6.0, 6.0).astype(jnp.bfloat16)


def draw_reply_query(key, part):
    key = jax.random.fold_in(key, 5)
    drawn = 2.0 * jax.random.normal(key, (RESPONSES * RESP_MAX, Q_HEADS * HD), jnp.float32)
    return jnp.clip(drawn, -7.0, 7.0).astype(jnp.bfloat16)


def draw_reply_key(key, part):
    key = jax.random.fold_in(key, 6)
    drawn = jax.random.normal(key, (RESPONSES * RESP_MAX, KV_HEADS * HD), jnp.float32)
    return jnp.clip(drawn, -6.0, 6.0).astype(jnp.bfloat16)


def with_ends(values, key, low, high):
    index_at = [jax.random.randint(jax.random.fold_in(key, axis), (), 0, length) for axis, length in enumerate(values.shape)]
    widest = values.shape.index(max(values.shape))
    neighbour = index_at[:widest] + [(index_at[widest] + 1) % values.shape[widest]] + index_at[widest + 1:]
    return values.at[tuple(index_at)].set(low).at[tuple(neighbour)].set(high)


def shard_levels(own_key, dims, split, smallest, largest):
    def one(axis_at, shards_of):
        draws = jax.random.uniform(jax.random.fold_in(jax.random.fold_in(own_key, 6), axis_at), (shards_of,), jnp.float32, smallest / len(split), largest / len(split))
        return jnp.repeat(jnp.exp(draws), dims[axis_at] // shards_of).reshape((-1,) + (1,) * (len(dims) - axis_at - 1))

    factor_of = one(*split[0])
    for cut in split[1:]:
        factor_of = factor_of * one(*cut)
    return factor_of


def length_profile(number_of, total, reach, skew):
    portions = [(1 << 20) // math.isqrt(standing ** skew) + 1 for standing in range(2, number_of + 1)]
    rest, given = total - reach - (number_of - 1), [1] * (number_of - 1)
    while rest > 0:
        free = [i for i in range(number_of - 1) if given[i] < reach]
        pool, remaining = sum([portions[i] for i in free]), rest
        for i in free:
            more = min(reach - given[i], max(1, remaining * portions[i] // pool), rest)
            given[i] = given[i] + more
            rest = rest - more
    return np.array([reach] + given)


def ragged(key, number_of, total, limit, lean):
    if number_of == 2:
        one = jax.random.randint(key, (), max(1, total - limit), min(limit, total - 1) + 1)
        return jnp.stack([one, total - one])
    tallies = jnp.asarray(length_profile(number_of, total, limit, lean), jnp.int32)
    pairs = (number_of - 1) // 2
    giver, sink = tallies[1:1 + 2 * pairs:2], tallies[2:2 + 2 * pairs:2]
    margin = jnp.minimum(giver - 1, limit - sink)
    moved = jax.random.randint(jax.random.fold_in(key, 1), (pairs,), 0, 1 << 20) % (margin + 1)
    tallies = tallies.at[1:1 + 2 * pairs:2].set(giver - moved).at[2:2 + 2 * pairs:2].set(sink + moved)
    return tallies[jax.random.permutation(jax.random.fold_in(key, 2), number_of)]


def gaussian(stream_key, shape, spread, limit, split=(), held_as=jnp.bfloat16):
    result = jax.random.normal(stream_key, shape, jnp.float32) * spread
    if len(split) > 0:
        result = shard_levels(stream_key, shape, split, -0.22, 0.18) * result
    return jnp.clip(result, min=-limit, max=limit).astype(held_as)


def setup_inputs(seed: int = 0) -> dict:
    streams_of = jax.random.split(jax.random.key(seed), 11)
    return {
        "prefix_query": draw_prefix_query(jax.random.fold_in(streams_of[10], 71), 0),
        "prefix_key": draw_prefix_key(jax.random.fold_in(streams_of[10], 71), 0),
        "prefix_value": gaussian(streams_of[2], (PREFIX_ROWS, KV_HEADS * HD), 1.0, 6.0, ((0, 256),)),
        "prefix_cotangent": gaussian(streams_of[3], (PREFIX_ROWS, Q_HEADS * HD), 1.0, 6.0, ((0, 256),)),
        "reply_query": draw_reply_query(jax.random.fold_in(streams_of[10], 71), 0),
        "reply_key": draw_reply_key(jax.random.fold_in(streams_of[10], 71), 0),
        "reply_value": gaussian(streams_of[6], (RESPONSES * RESP_MAX, KV_HEADS * HD), 1.0, 6.0, ((0, 64), (1, 4))),
        "reply_cotangent": gaussian(streams_of[7], (RESPONSES * RESP_MAX, Q_HEADS * HD), 1.0, 6.0, ((0, 64), (1, 4))),
        "parent": with_ends(jax.random.randint(streams_of[8], (RESPONSES,), 0, PROMPTS), jax.random.fold_in(streams_of[8], 1), 0, PROMPTS - 1).astype(jnp.int32),
        "lengths": ragged(streams_of[9], RESPONSES, RESPONSES * RESP_MAX * 5 // 8, RESP_MAX, 1).astype(jnp.int32),
    }


def keep_half(tensor):
    return lax.optimization_barrier(tensor.astype(jnp.bfloat16)).astype(jnp.float32)

def head_pass(operands, visible, live_float):
    query_head, cotan_head, key_head, value_head = operands
    score_scale = 1.0 / math.sqrt(HD)
    scores = jnp.einsum('rnd,kd->nrk', query_head, key_head) * score_scale
    scores = jnp.where(visible[None], scores, -jnp.inf)
    row_max = lax.optimization_barrier(jnp.max(scores, axis=2, keepdims=True))
    log_total = row_max + jnp.log(lax.optimization_barrier(jnp.sum(jnp.exp(scores - row_max), axis=2, keepdims=True)))
    weights = jnp.exp(scores - log_total) * live_float[None, :, None]
    weights_half = keep_half(weights)
    output_half = keep_half(jnp.einsum('nrk,kd->rnd', weights_half, value_head))
    row_dot = jnp.einsum('rnd,rnd->nr', output_half, cotan_head)[:, :, None]
    weight_grad = jnp.einsum('rnd,kd->nrk', cotan_head, value_head)
    score_grad = keep_half(weights * (weight_grad - row_dot))
    query_grad = jnp.einsum('nrk,kd->rnd', score_grad, key_head) * score_scale
    key_grad = jnp.einsum('nrk,rnd->kd', score_grad, query_head) * score_scale
    value_grad = jnp.einsum('nrk,rnd->kd', weights_half, cotan_head)
    return (output_half, query_grad, key_grad, value_grad)

def attention_pass(query, cotangent, key_set, value_set, visible, live_rows):
    row_count = query.shape[0]
    key_count = key_set.shape[0]
    query_heads = query.astype(jnp.float32).reshape(row_count, KV_HEADS, GROUP, HD).transpose(1, 0, 2, 3)
    cotan_heads = cotangent.astype(jnp.float32).reshape(row_count, KV_HEADS, GROUP, HD).transpose(1, 0, 2, 3)
    key_heads = key_set.astype(jnp.float32).reshape(key_count, KV_HEADS, HD).transpose(1, 0, 2)
    value_heads = value_set.astype(jnp.float32).reshape(key_count, KV_HEADS, HD).transpose(1, 0, 2)
    live_float = live_rows.astype(jnp.float32)
    output_half, query_grad, key_grad, value_grad = lax.map(lambda operands: head_pass(operands, visible, live_float), (query_heads, cotan_heads, key_heads, value_heads))
    output = output_half.transpose(1, 0, 2, 3).reshape(row_count, -1).astype(jnp.bfloat16)
    query_grad = query_grad.transpose(1, 0, 2, 3).reshape(row_count, -1)
    key_grad = key_grad.transpose(1, 0, 2).reshape(key_count, -1)
    value_grad = value_grad.transpose(1, 0, 2).reshape(key_count, -1)
    return (output, query_grad, key_grad, value_grad)

def reference(prefix_query, prefix_key, prefix_value, prefix_cotangent, reply_query, reply_key, reply_value, reply_cotangent, parent, lengths):
    positions = jnp.arange(PREFIX_LEN, dtype=jnp.int32)
    causal = positions[:, None] >= positions[None, :]
    everyone = jnp.ones((PREFIX_LEN,), jnp.bool_)
    prefix_parts = []
    for prompt in range(PROMPTS):
        first_row = prompt * PREFIX_LEN
        last_row = first_row + PREFIX_LEN
        prefix_parts.append(attention_pass(prefix_query[first_row:last_row], prefix_cotangent[first_row:last_row], prefix_key[first_row:last_row], prefix_value[first_row:last_row], causal, everyone))
    slot_index = jnp.arange(RESP_MAX, dtype=jnp.int32)
    reply_visible = jnp.concatenate([jnp.ones((RESP_MAX, PREFIX_LEN), jnp.bool_), slot_index[:, None] >= slot_index[None, :]], axis=1)

    def one_reply(totals, operands):
        key_total, value_total = totals
        query_rows, key_rows, value_rows, cotan_rows, source, length = operands
        offset = (source * PREFIX_LEN).astype(jnp.int32)
        key_set = jnp.concatenate([lax.dynamic_slice_in_dim(prefix_key, offset, PREFIX_LEN, 0), key_rows], axis=0)
        value_set = jnp.concatenate([lax.dynamic_slice_in_dim(prefix_value, offset, PREFIX_LEN, 0), value_rows], axis=0)
        output, query_grad, key_grad, value_grad = attention_pass(query_rows, cotan_rows, key_set, value_set, reply_visible, slot_index < length)
        key_total = lax.dynamic_update_slice_in_dim(key_total, lax.dynamic_slice_in_dim(key_total, offset, PREFIX_LEN, 0) + key_grad[:PREFIX_LEN], offset, 0)
        value_total = lax.dynamic_update_slice_in_dim(value_total, lax.dynamic_slice_in_dim(value_total, offset, PREFIX_LEN, 0) + value_grad[:PREFIX_LEN], offset, 0)
        return ((key_total, value_total), (output, query_grad.astype(jnp.bfloat16), key_grad[PREFIX_LEN:].astype(jnp.bfloat16), value_grad[PREFIX_LEN:].astype(jnp.bfloat16)))
    kv_width = KV_HEADS * HD
    start_totals = (jnp.zeros((PREFIX_ROWS, kv_width), jnp.float32), jnp.zeros((PREFIX_ROWS, kv_width), jnp.float32))
    operands = (reply_query.reshape(RESPONSES, RESP_MAX, -1), reply_key.reshape(RESPONSES, RESP_MAX, -1), reply_value.reshape(RESPONSES, RESP_MAX, -1), reply_cotangent.reshape(RESPONSES, RESP_MAX, -1), parent, lengths)
    final_totals, reply_parts = lax.scan(one_reply, start_totals, operands)
    prefix_output = jnp.concatenate([portion[0] for portion in prefix_parts], axis=0)
    prefix_query_gradient = jnp.concatenate([portion[1] for portion in prefix_parts], axis=0).astype(jnp.bfloat16)
    prefix_key_gradient = (jnp.concatenate([portion[2] for portion in prefix_parts], axis=0) + final_totals[0]).astype(jnp.bfloat16)
    prefix_value_gradient = (jnp.concatenate([portion[3] for portion in prefix_parts], axis=0) + final_totals[1]).astype(jnp.bfloat16)
    reply_output = reply_parts[0].reshape(RESPONSES * RESP_MAX, -1)
    reply_query_gradient = reply_parts[1].reshape(RESPONSES * RESP_MAX, -1)
    reply_key_gradient = reply_parts[2].reshape(RESPONSES * RESP_MAX, -1)
    reply_value_gradient = reply_parts[3].reshape(RESPONSES * RESP_MAX, -1)
    return (prefix_output, prefix_query_gradient, prefix_key_gradient, prefix_value_gradient, reply_output, reply_query_gradient, reply_key_gradient, reply_value_gradient)
```

```python
import functools
import math

import jax
import jax.numpy as jnp
from jax import lax
from jax.experimental import pallas as pl
from jax.experimental.pallas import tpu as pltpu
from jax.sharding import Mesh, PartitionSpec as P
HD=128; GROUP=8; LEN=1024; SLOTS=256; ROWS=64; M=ROWS*GROUP
SCALE=1.0/math.sqrt(HD); LOG2E=math.log2(math.e)
NT=(((1,),(1,)),((),())); NN=(((1,),(0,)),((),()))
def dot(a,b,dims=NN): return lax.dot_general(a,b,dims,preferred_element_type=jnp.float32)
def stack(x): return jnp.concatenate([x[:,h*HD:(h+1)*HD] for h in range(GROUP)],axis=0)
def unstack(x): return jnp.concatenate([x[h*ROWS:(h+1)*ROWS] for h in range(GROUP)],axis=1)
def tr(x): return x.astype(jnp.float32).T.astype(jnp.bfloat16)

def pieces(q,do,parts,live):
    raw=[]
    for key,val,vis in parts:
        s=dot(q,key,NT)
        if vis is not None: s=jnp.where(vis,s,-1e30)
        raw.append(s)
    m=functools.reduce(jnp.maximum,[jnp.max(s,axis=1,keepdims=True) for s in raw])
    c=SCALE*LOG2E
    mc=m*c
    w=[jnp.exp2(s*c-mc) for s in raw]
    wh=[x.astype(jnp.bfloat16) for x in w]
    oe=functools.reduce(jnp.add,[dot(x,val) for x,(key,val,vis) in zip(wh,parts)])
    inv=1.0/oe[:,HD:]
    if live is not None: inv=inv*live
    o=(oe[:,:HD]*inv).astype(jnp.bfloat16)
    dof=do.astype(jnp.float32)
    dos=dof*inv
    rd=jnp.sum(o.astype(jnp.float32)*dos,axis=1,keepdims=True)
    hi=(-rd).astype(jnp.bfloat16).astype(jnp.float32)
    lo=-rd-hi
    lane=lax.broadcasted_iota(jnp.int32,(M,HD),1)
    ext=jnp.where(lane==0,hi,jnp.where(lane==1,lo,0.0)).astype(jnp.bfloat16)
    dob=dos.astype(jnp.bfloat16)
    doe=jnp.concatenate([dob,ext],axis=1)
    qT=tr(q); doT=dos.T.astype(jnp.bfloat16)
    dq=None; grads=[]
    for x,xh,(key,val,vis) in zip(w,wh,parts):
        dp=dot(doe,val,NT)
        ds=(x*dp).astype(jnp.bfloat16)
        t=dot(ds,key); dq=t if dq is None else dq+t
        grads.append((dot(qT,ds),dot(doT,xh)))
    return o,(dq*SCALE).astype(jnp.bfloat16),grads

def kernel(info,qa,da,qb,db,qp,dp_,k,v,ka,va,kb,vb,
           oa,ga,ob,gb,op,gp,kvg,owna,ownb, kT,vT,okT,ovT):
    u=pl.program_id(0)
    @pl.when(u==0)
    def _():
        kT[...]=jnp.zeros_like(kT); vT[...]=jnp.zeros_like(vT)
    r=u//4; b=u%4
    ones=lambda n: jnp.ones((n,HD),jnp.bfloat16)
    def reply(slot,q_ref,d_ref,ko,vo,o_ref,g_ref,own_ref):
        length=info[2+slot]; source=info[slot]
        @pl.when(b==0)
        def _():
            okT[...]=jnp.zeros_like(okT); ovT[...]=jnp.zeros_like(ovT)
        alive=b*ROWS<length
        @pl.when(jnp.logical_not(alive))
        def _():
            o_ref[...]=jnp.zeros_like(o_ref); g_ref[...]=jnp.zeros_like(g_ref)
        @pl.when(alive)
        def _():
            q=stack(q_ref[...]); d=stack(d_ref[...])
            off=pl.multiple_of(source*LEN,LEN)
            key=k[pl.ds(off,LEN),:]; val=jnp.concatenate([v[pl.ds(off,LEN),:],ones(LEN)],axis=1)
            valo=jnp.concatenate([vo[...],ones(SLOTS)],axis=1)
            row=b*ROWS+lax.broadcasted_iota(jnp.int32,(M,1),0)%ROWS
            vis=row>=lax.broadcasted_iota(jnp.int32,(M,SLOTS),1)
            live=(row<length).astype(jnp.float32)
            o,dq,gr=pieces(q,d,[(key,val,None),(ko[...],valo,vis)],live)
            o_ref[...]=unstack(o); g_ref[...]=unstack(dq)
            kT[:,pl.ds(off,LEN)]+=gr[0][0]; vT[:,pl.ds(off,LEN)]+=gr[0][1]
            okT[...]+=gr[1][0]; ovT[...]+=gr[1][1]
        @pl.when(b==3)
        def _():
            own_ref[:,:HD]=(okT[...]*SCALE).T.astype(jnp.bfloat16)
            own_ref[:,HD:]=ovT[...].T.astype(jnp.bfloat16)
    @pl.when(r==0)
    def _(): reply(0,qa,da,ka,va,oa,ga,owna)
    @pl.when(r==1)
    def _(): reply(1,qb,db,kb,vb,ob,gb,ownb)
    @pl.when(u==8)
    def _():
        q=stack(qp[...]); d=stack(dp_[...])
        off=pl.multiple_of(info[5]*LEN,LEN)
        key=k[pl.ds(off,LEN),:]; val=jnp.concatenate([v[pl.ds(off,LEN),:],ones(LEN)],axis=1)
        row=info[6]+lax.broadcasted_iota(jnp.int32,(M,1),0)%ROWS
        vis=row>=lax.broadcasted_iota(jnp.int32,(M,LEN),1)
        o,dq,gr=pieces(q,d,[(key,val,vis)],None)
        op[...]=unstack(o); gp[...]=unstack(dq)
        kT[:,pl.ds(off,LEN)]+=gr[0][0]; vT[:,pl.ds(off,LEN)]+=gr[0][1]
        kvg[:,:HD]=(kT[...]*SCALE).T.astype(jnp.bfloat16)
        kvg[:,HD:]=vT[...].T.astype(jnp.bfloat16)

def call(info,qa,da,qb,db,qp,dp_,k,v,ka,va,kb,vb):
    bf=jnp.bfloat16; G=GROUP*HD
    ia=lambda u,s:(jnp.minimum(u,3),s[4]); ib=lambda u,s:(jnp.clip(u-4,0,3),0); z=lambda u,s:(0,0)
    full=lambda a: pl.BlockSpec(a.shape,z)
    S=jax.ShapeDtypeStruct
    return pl.pallas_call(kernel,
        grid_spec=pltpu.PrefetchScalarGridSpec(num_scalar_prefetch=1,grid=(9,),
            in_specs=[pl.BlockSpec((ROWS,G),ia)]*2+[pl.BlockSpec((ROWS,G),ib)]*2+[full(qp),full(dp_),full(k),full(v),full(ka),full(va),full(kb),full(vb)],
            out_specs=[pl.BlockSpec((ROWS,G),ia)]*2+[pl.BlockSpec((ROWS,G),ib)]*2+[pl.BlockSpec((ROWS,G),z)]*2+[pl.BlockSpec((2*LEN,2*HD),z),pl.BlockSpec((SLOTS,2*HD),z),pl.BlockSpec((SLOTS,2*HD),z)],
            scratch_shapes=[pltpu.VMEM((HD,2*LEN),jnp.float32)]*2+[pltpu.VMEM((HD,SLOTS),jnp.float32)]*2),
        out_shape=[S((SLOTS,2*G),bf),S((SLOTS,2*G),bf),S((SLOTS,G),bf),S((SLOTS,G),bf),S((ROWS,G),bf),S((ROWS,G),bf),S((2*LEN,2*HD),bf),S((SLOTS,2*HD),bf),S((SLOTS,2*HD),bf)],
        compiler_params=pltpu.CompilerParams(vmem_limit_bytes=56*1024*1024),
        name="attn")(info,qa,da,qb,db,qp,dp_,k,v,ka,va,kb,vb)


ALL=("x","z","core","head")
PAIR=("core","head")

def exchange(v,axes): return lax.all_to_all(v,axes,split_axis=0,concat_axis=0,tiled=True)
def swap(v): return lax.ppermute(v,"core",[(0,1),(1,0)])
def by_head(v,width):
    return v.reshape(8,4,2,width).transpose(2,1,0,3).reshape(8,8,width)
def to_rows(v,width):
    return v.reshape(2,4,8,width).transpose(2,1,0,3).reshape(8,8*width)

def shards(pq,pk,pv,pd,rq,rk,rv,rd,parent,lengths):
    x=lax.axis_index("x"); z=lax.axis_index("z"); core=lax.axis_index("core")
    G=GROUP*HD
    kv=jnp.concatenate([by_head(pk,HD),by_head(pv,HD)],axis=2)
    kv=jnp.broadcast_to(kv[None],(32,8,8,2*HD)).reshape(256,8,2*HD)
    kv=exchange(kv,ALL).reshape(32,8,8,2*HD)
    kv=kv.reshape(2*LEN,2*HD)
    qd=exchange(jnp.concatenate([by_head(pq,G),by_head(pd,G)],axis=2),PAIR).reshape(ROWS,2*G)
    other=1-core
    far=lambda v,w: swap(lax.dynamic_slice_in_dim(v,other*w,w,1))
    near=lambda v,w: lax.dynamic_slice_in_dim(v,core*w,w,1)
    qb,db,kb,vb=far(rq,G),far(rd,G),far(rk,HD),far(rv,HD)
    ka,va=near(rk,HD),near(rv,HD)
    mine=jnp.concatenate([parent,lengths])
    theirs=swap(mine)
    row=(x*8+z)*ROWS
    prompt=row//LEN
    info=jnp.stack([mine[0],theirs[0],mine[1],theirs[1],core,prompt,row-prompt*LEN,core]).astype(jnp.int32)
    oa,ga,ob,gb,op,gp,kvg,owna,ownb=call(info,rq,rd,qb,db,qd[:,:G],qd[:,G:],kv[:,:HD],kv[:,HD:],ka,va,kb,vb)
    ob,gb,ownb=swap(ob),swap(gb),swap(ownb)
    ro=lax.dynamic_update_slice_in_dim(oa,ob,other*G,1)
    rg=lax.dynamic_update_slice_in_dim(ga,gb,other*G,1)
    first=jnp.where(core==0,owna,ownb); second=jnp.where(core==0,ownb,owna)
    rkg=jnp.concatenate([first[:,:HD],second[:,:HD]],axis=1)
    rvg=jnp.concatenate([first[:,HD:],second[:,HD:]],axis=1)
    tot=exchange(kvg.reshape(256,8,2*HD),ALL).reshape(32,8,8,2*HD).astype(jnp.float32).sum(0).astype(jnp.bfloat16)
    back=exchange(jnp.concatenate([op.reshape(8,8,G),gp.reshape(8,8,G)],axis=2),PAIR)
    return (to_rows(back[:,:,:G],G),to_rows(back[:,:,G:],G),to_rows(tot[:,:,:HD],HD),to_rows(tot[:,:,HD:],HD),ro,rg,rkg,rvg)

def solution(mesh):
    fine=Mesh(mesh.devices.reshape(4,8,2,4),ALL)
    ctx=("x","z","core")
    rows=P(ALL,None); cols=P(ctx,"head")
    return jax.shard_map(shards,mesh=fine,in_specs=(rows,)*4+(cols,)*4+(P(ctx),)*2,out_specs=(rows,)*4+(cols,)*4,check_vma=False)
```

```python
import functools
import math

import jax
import jax.numpy as jnp
from jax import lax
from jax.experimental import pallas as pl
from jax.experimental.pallas import tpu as pltpu
from jax.sharding import Mesh, PartitionSpec as P
HD=128; GROUP=8; LEN=1024; SLOTS=256; ROWS=64; M=ROWS*GROUP; SLAB=512
SCALE=1.0/math.sqrt(HD); LOG2E=math.log2(math.e)
NT=(((1,),(1,)),((),())); NN=(((1,),(0,)),((),()))
def dot(a,b,dims=NN): return lax.dot_general(a,b,dims,preferred_element_type=jnp.float32)
def stack(x): return jnp.concatenate([x[:,h*HD:(h+1)*HD] for h in range(GROUP)],axis=0)
def unstack(x): return jnp.concatenate([x[h*ROWS:(h+1)*ROWS] for h in range(GROUP)],axis=1)
F=jnp.float32; H=jnp.bfloat16
def tr(x): return x.astype(F).T.astype(H)

class Block: pass

def scores(t):
    t.s=[dot(t.q,key,NT) if vis is None else jnp.where(vis,dot(t.q,key,NT),-1e30) for key,val,vis in t.parts]

def softmax(t):
    m=functools.reduce(jnp.maximum,[jnp.max(s,axis=1,keepdims=True) for s in t.s])
    c=SCALE*LOG2E
    mc=m*c
    t.w=[jnp.exp2(s*c-mc) for s in t.s]
    t.wh=[x.astype(H) for x in t.w]

def output(t):
    oe=functools.reduce(jnp.add,[dot(x,part[1]) for x,part in zip(t.wh,t.parts)])
    inv=1.0/oe[:,HD:]
    if t.live is not None: inv=inv*t.live
    t.o=(oe[:,:HD]*inv).astype(H)
    dos=t.do.astype(F)*inv
    rd=jnp.sum(t.o.astype(F)*dos,axis=1,keepdims=True)
    hi=(-rd).astype(H).astype(F)
    lo=-rd-hi
    lane=lax.broadcasted_iota(jnp.int32,(t.q.shape[0],HD),1)
    ext=jnp.where(lane==0,hi,jnp.where(lane==1,lo,0.0)).astype(H)
    t.dE=jnp.concatenate([dos.astype(H),ext],axis=1)
    t.dT=dos.T.astype(H)
    t.qT=tr(t.q)

def score_grad(t):
    t.ds=[(x*dot(t.dE,part[1],NT)).astype(H) for x,part in zip(t.w,t.parts)]

def query_grad(t):
    t.dq=(functools.reduce(jnp.add,[dot(x,part[0]) for x,part in zip(t.ds,t.parts)])*SCALE).astype(H)

def pieces(q,do,parts,live):
    halves=[]
    for i in range(2):
        cut=lambda v: None if v is None else v[i*M//2:(i+1)*M//2]
        t=Block(); t.q=cut(q); t.do=cut(do); t.live=cut(live)
        t.parts=[(key,val,cut(vis)) for key,val,vis in parts]
        halves.append(t)
    for step in (scores,softmax,output,score_grad,query_grad):
        for t in halves: step(t)
    a,b=halves
    dvs=[dot(a.dT,x)+dot(b.dT,y) for x,y in zip(a.wh,b.wh)]
    dks=[dot(a.qT,x)+dot(b.qT,y) for x,y in zip(a.ds,b.ds)]
    return jnp.concatenate([a.o,b.o]),jnp.concatenate([a.dq,b.dq]),list(zip(dks,dvs))

HALF=SLAB//2
def slab_at(x,d): return pl.multiple_of(lax.rem(x+d,4)*SLAB,SLAB)

def kernel(info,qa,da,qb,db,qd,s0,s1,s2,s3,ka,va,kb,vb,
           oa,ga,ob,gb,og,g0,g1,g2,g3,g4,owna,ownb, kg,vg,okg,ovg,ks,vs):
    u=pl.program_id(0); x=info[7]
    @pl.when(u==0)
    def _():
        kg[...]=jnp.zeros_like(kg); vg[...]=jnp.zeros_like(vg)
        vs[:,HD:]=jnp.ones((2*LEN,HD),H)
        for ref,d,first in ((s0,0,0),(s1,3,0),(s2,1,0),(s3,2,0)):
            n=ref.shape[0]; at=slab_at(x,d)+first
            ks[pl.ds(at,n),:]=ref[:,:HD]
            vs[pl.ds(at,n),:HD]=ref[:,HD:]
    r=u//4; b=u%4
    def add(off,g):
        kg[:,pl.ds(off,LEN)]+=g[0]; vg[:,pl.ds(off,LEN)]+=g[1]
    def prompt(source):
        off=pl.multiple_of(source*LEN,LEN)
        return off,(ks[pl.ds(off,LEN),:],vs[pl.ds(off,LEN),:])
    def reply(slot,q_ref,d_ref,ko,vo,o_ref,g_ref,own_ref):
        length=info[2+slot]; source=info[slot]
        @pl.when(b==0)
        def _():
            okg[...]=jnp.zeros_like(okg); ovg[...]=jnp.zeros_like(ovg)
        alive=b*ROWS<length
        @pl.when(jnp.logical_not(alive))
        def _():
            o_ref[...]=jnp.zeros_like(o_ref); g_ref[...]=jnp.zeros_like(g_ref)
        @pl.when(alive)
        def _():
            off,main=prompt(source)
            row=b*ROWS+lax.broadcasted_iota(jnp.int32,(M,1),0)%ROWS
            vis=row>=lax.broadcasted_iota(jnp.int32,(M,SLOTS),1)
            live=(row<length).astype(F)
            o,dq,g=pieces(stack(q_ref[...]),stack(d_ref[...]),[main+(None,),(ko[...],jnp.concatenate([vo[...],jnp.ones((SLOTS,HD),H)],axis=1),vis)],live)
            o_ref[...]=unstack(o); g_ref[...]=unstack(dq)
            add(off,g[0])
            okg[...]+=g[1][0]; ovg[...]+=g[1][1]
        @pl.when(b==3)
        def _():
            own_ref[:,:HD]=(okg[...]*SCALE).T.astype(H)
            own_ref[:,HD:]=ovg[...].T.astype(H)
    @pl.when(r==0)
    def _(): reply(0,qa,da,ka,va,oa,ga,owna)
    @pl.when(r==1)
    def _(): reply(1,qb,db,kb,vb,ob,gb,ownb)
    @pl.when(u==8)
    def _():
        off,main=prompt(info[5])
        row=info[6]+lax.broadcasted_iota(jnp.int32,(M,1),0)%ROWS
        vis=row>=lax.broadcasted_iota(jnp.int32,(M,LEN),1)
        o,dq,g=pieces(stack(qd[:,:G]),stack(qd[:,G:]),[main+(vis,)],None)
        og[:,:G]=unstack(o); og[:,G:]=unstack(dq)
        add(off,g[0])
        for ref,d,first in ((g0,0,0),(g1,1,0),(g2,3,0),(g3,2,0),(g4,2,HALF)):
            n=ref.shape[0]; at=slab_at(x,d)+first
            ref[:,:HD]=(kg[:,pl.ds(at,n)]*SCALE).T.astype(H)
            ref[:,HD:]=vg[:,pl.ds(at,n)].T.astype(H)

G=GROUP*HD
def call(info,qa,da,qb,db,qd,slabs,ka,va,kb,vb):
    near=pl.BlockSpec((ROWS,G),lambda u,s:(jnp.minimum(u,3),s[4]))
    far=pl.BlockSpec((ROWS,G),lambda u,s:(jnp.clip(u-4,0,3),0))
    full=lambda *shape: pl.BlockSpec(shape,lambda u,s:(0,0))
    half=pl.BlockSpec((SLOTS,HD),lambda u,s:(0,s[4]))
    out=lambda *shape: jax.ShapeDtypeStruct(shape,H)
    whole=full(SLAB,2*HD); part=full(HALF,2*HD); own=full(SLOTS,2*HD)
    scratch=[(HD,2*LEN,F),(HD,2*LEN,F),(HD,SLOTS,F),(HD,SLOTS,F),(2*LEN,HD,H),(2*LEN,2*HD,H)]
    return pl.pallas_call(kernel,
        grid_spec=pltpu.PrefetchScalarGridSpec(num_scalar_prefetch=1,grid=(9,),
            in_specs=[near,near,far,far,full(ROWS,2*G)]+[whole]*4+[half,half]+[full(SLOTS,HD)]*2,
            out_specs=[near,near,far,far,full(ROWS,2*G)]+[whole]*3+[part]*2+[own]*2,
            scratch_shapes=[pltpu.VMEM(s[:2],s[2]) for s in scratch]),
        out_shape=[out(SLOTS,2*G),out(SLOTS,2*G),out(SLOTS,G),out(SLOTS,G),out(ROWS,2*G)]+[out(SLAB,2*HD)]*3+[out(HALF,2*HD)]*2+[out(SLOTS,2*HD)]*2,
        compiler_params=pltpu.CompilerParams(vmem_limit_bytes=56*1024*1024),
        name="attn")(info,qa,da,qb,db,qd,*slabs,ka,va,kb,vb)

ALL=("x","z","core","head")
PLANE=("z","core","head")
PAIR=("core","head")

def exchange(v,axes): return lax.all_to_all(v,axes,split_axis=0,concat_axis=0,tiled=True)
def swap(v): return lax.ppermute(v,"core",[(0,1),(1,0)])
def shift(v,d): return lax.ppermute(v,"x",[(i,(i+d)%4) for i in range(4)])
def by_head(v,width):
    return v.reshape(8,4,2,width).transpose(2,1,0,3).reshape(8,8,width)
def to_rows(v,width):
    return v.reshape(2,4,8,width).transpose(2,1,0,3).reshape(8,8*width)

def shards(pq,pk,pv,pd,rq,rk,rv,rd,parent,lengths):
    x=lax.axis_index("x"); z=lax.axis_index("z"); core=lax.axis_index("core")
    kv=jnp.concatenate([by_head(pk,HD),by_head(pv,HD)],axis=2)
    kv=jnp.broadcast_to(kv[None],(8,8,8,2*HD)).reshape(64,8,2*HD)
    slab=exchange(kv,PLANE).reshape(SLAB,2*HD)
    slabs=(slab,shift(slab,1),shift(slab,3),shift(slab,2))
    other=1-core
    far=lambda v,w: swap(lax.dynamic_slice_in_dim(v,other*w,w,1))
    kb,vb=far(rk,HD),far(rv,HD)
    qb,db=far(rq,G),far(rd,G)
    theirs=swap(jnp.concatenate([parent,lengths]))
    qd=exchange(jnp.concatenate([by_head(pq,G),by_head(pd,G)],axis=2),PAIR).reshape(ROWS,2*G)
    row=(x*8+z)*ROWS
    prompt=row//LEN
    at=lax.broadcasted_iota(jnp.int32,(8,),0)
    info=jnp.zeros((8,),jnp.int32)
    for i,v in enumerate((parent[0],theirs[0],lengths[0],theirs[1],core,prompt,row-prompt*LEN,x)):
        info=jnp.where(at==i,v,info)
    oa,ga,ob,gb,og,g0,g1,g2,g3,g4,owna,ownb=call(info,rq,rd,qb,db,qd,slabs,rk,rv,kb,vb)
    g4=shift(shift(g4,3),3)
    opposite=jnp.concatenate([shift(g3,2),g4],axis=0)
    part=(g0.astype(F)+shift(g1,1).astype(F)+shift(g2,3).astype(F)+opposite.astype(F)).astype(H)
    ownb=swap(ownb)
    og,ownb=lax.optimization_barrier((og,ownb))
    back=exchange(og.reshape(8,8,2*G),PAIR)
    back,part=lax.optimization_barrier((back,part))
    tot=exchange(part.reshape(64,8,2*HD),PLANE).reshape(8,8,8,2*HD).astype(F).sum(0).astype(H)
    ob,gb=swap(ob),swap(gb)
    ro=lax.dynamic_update_slice_in_dim(oa,ob,other*G,1)
    rg=lax.dynamic_update_slice_in_dim(ga,gb,other*G,1)
    first=jnp.where(core==0,owna,ownb); second=jnp.where(core==0,ownb,owna)
    rkg=jnp.concatenate([first[:,:HD],second[:,:HD]],axis=1)
    rvg=jnp.concatenate([first[:,HD:],second[:,HD:]],axis=1)
    return (to_rows(back[:,:,:G],G),to_rows(back[:,:,G:],G),to_rows(tot[:,:,:HD],HD),to_rows(tot[:,:,HD:],HD),ro,rg,rkg,rvg)

def solution(mesh):
    fine=Mesh(mesh.devices.reshape(4,8,2,4),ALL)
    ctx=("x","z","core")
    rows=P(ALL,None); cols=P(ctx,"head")
    return jax.shard_map(shards,mesh=fine,in_specs=(rows,)*4+(cols,)*4+(P(ctx),)*2,out_specs=(rows,)*4+(cols,)*4,check_vma=False)
```

```python
import functools
import math

import jax
import jax.numpy as jnp
from jax import lax
from jax.experimental import pallas as pl
from jax.experimental.pallas import tpu as pltpu
from jax.sharding import Mesh, PartitionSpec as P
HD=128; GROUP=8; LEN=1024; SLOTS=256; ROWS=64; M=ROWS*GROUP; SLAB=512
SCALE=1.0/math.sqrt(HD); LOG2E=math.log2(math.e)
NT=(((1,),(1,)),((),())); NN=(((1,),(0,)),((),()))
def dot(a,b,dims=NN): return lax.dot_general(a,b,dims,preferred_element_type=jnp.float32)
def stack(x): return jnp.concatenate([x[:,h*HD:(h+1)*HD] for h in range(GROUP)],axis=0)
def unstack(x): return jnp.concatenate([x[h*ROWS:(h+1)*ROWS] for h in range(GROUP)],axis=1)
F=jnp.float32; H=jnp.bfloat16
def tr(x): return x.astype(F).T.astype(H)

class Block: pass

def scores(t):
    t.s=[dot(t.q,key,NT) if vis is None else jnp.where(vis,dot(t.q,key,NT),-1e30) for key,val,vis in t.parts]

def softmax(t):
    m=functools.reduce(jnp.maximum,[jnp.max(s,axis=1,keepdims=True) for s in t.s])
    c=SCALE*LOG2E
    mc=m*c
    t.w=[jnp.exp2(s*c-mc) for s in t.s]
    t.wh=[x.astype(H) for x in t.w]

def output(t):
    oe=functools.reduce(jnp.add,[dot(x,part[1]) for x,part in zip(t.wh,t.parts)])
    inv=1.0/oe[:,HD:]
    if t.live is not None: inv=inv*t.live
    t.o=(oe[:,:HD]*inv).astype(H)
    dos=t.do.astype(F)*inv
    rd=jnp.sum(t.o.astype(F)*dos,axis=1,keepdims=True)
    hi=(-rd).astype(H).astype(F)
    lo=-rd-hi
    lane=lax.broadcasted_iota(jnp.int32,(t.q.shape[0],HD),1)
    ext=jnp.where(lane==0,hi,jnp.where(lane==1,lo,0.0)).astype(H)
    t.dE=jnp.concatenate([dos.astype(H),ext],axis=1)
    t.dT=dos.T.astype(H)
    t.qT=tr(t.q)

def score_grad(t):
    t.ds=[(x*dot(t.dE,part[1],NT)).astype(H) for x,part in zip(t.w,t.parts)]

def query_grad(t):
    t.dq=(functools.reduce(jnp.add,[dot(x,part[0]) for x,part in zip(t.ds,t.parts)])*SCALE).astype(H)

def pieces(q,do,parts,live):
    halves=[]
    for i in range(2):
        cut=lambda v: None if v is None else v[i*M//2:(i+1)*M//2]
        t=Block(); t.q=cut(q); t.do=cut(do); t.live=cut(live)
        t.parts=[(key,val,cut(vis)) for key,val,vis in parts]
        halves.append(t)
    for step in (scores,softmax,output,score_grad,query_grad):
        for t in halves: step(t)
    a,b=halves
    dvs=[dot(a.dT,x)+dot(b.dT,y) for x,y in zip(a.wh,b.wh)]
    dks=[dot(a.qT,x)+dot(b.qT,y) for x,y in zip(a.ds,b.ds)]
    return jnp.concatenate([a.o,b.o]),jnp.concatenate([a.dq,b.dq]),list(zip(dks,dvs))

HALF=SLAB//2
def slab_at(x,d): return pl.multiple_of(lax.rem(x+d,4)*SLAB,SLAB)

def kernel(info,qa,da,qb,db,qd,s0,s1,s2,s3,ka,va,kb,vb,
           oa,ga,ob,gb,og,g0,g1,g2,g3,g4,owna,ownb, kg,vg,okg,ovg,ks,vs):
    u=pl.program_id(0); x=info[7]
    @pl.when(u==0)
    def _():
        kg[...]=jnp.zeros_like(kg); vg[...]=jnp.zeros_like(vg)
        vs[:,HD:]=jnp.ones((2*LEN,HD),H)
        for ref,d,first in ((s0,0,0),(s1,3,0),(s2,1,0),(s3,2,0)):
            n=ref.shape[0]; at=slab_at(x,d)+first
            ks[pl.ds(at,n),:]=ref[:,:HD]
            vs[pl.ds(at,n),:HD]=ref[:,HD:]
    r=u//4; b=u%4
    def add(off,g):
        kg[:,pl.ds(off,LEN)]+=g[0]; vg[:,pl.ds(off,LEN)]+=g[1]
    def prompt(source):
        off=pl.multiple_of(source*LEN,LEN)
        return off,(ks[pl.ds(off,LEN),:],vs[pl.ds(off,LEN),:])
    def reply(slot,q_ref,d_ref,ko,vo,o_ref,g_ref,own_ref):
        length=info[2+slot]; source=info[slot]
        @pl.when(b==0)
        def _():
            okg[...]=jnp.zeros_like(okg); ovg[...]=jnp.zeros_like(ovg)
        alive=b*ROWS<length
        @pl.when(jnp.logical_not(alive))
        def _():
            o_ref[...]=jnp.zeros_like(o_ref); g_ref[...]=jnp.zeros_like(g_ref)
        def unit(seen):
            off,main=prompt(source)
            row=b*ROWS+lax.broadcasted_iota(jnp.int32,(M,1),0)%ROWS
            vis=row>=lax.broadcasted_iota(jnp.int32,(M,seen),1)
            live=(row<length).astype(F)
            val=jnp.concatenate([vo[:seen],jnp.ones((seen,HD),H)],axis=1)
            o,dq,g=pieces(stack(q_ref[...]),stack(d_ref[...]),[main+(None,),(ko[:seen],val,vis)],live)
            o_ref[...]=unstack(o); g_ref[...]=unstack(dq)
            add(off,g[0])
            okg[:,:seen]+=g[1][0]; ovg[:,:seen]+=g[1][1]
        @pl.when(jnp.logical_and(alive,b<2))
        def _(): unit(SLOTS//2)
        @pl.when(jnp.logical_and(alive,b>=2))
        def _(): unit(SLOTS)
        @pl.when(b==3)
        def _():
            own_ref[:,:HD]=(okg[...]*SCALE).T.astype(H)
            own_ref[:,HD:]=ovg[...].T.astype(H)
    @pl.when(r==0)
    def _(): reply(0,qa,da,ka,va,oa,ga,owna)
    @pl.when(r==1)
    def _(): reply(1,qb,db,kb,vb,ob,gb,ownb)
    @pl.when(u==8)
    def _():
        off,main=prompt(info[5])
        row=info[6]+lax.broadcasted_iota(jnp.int32,(M,1),0)%ROWS
        vis=row>=lax.broadcasted_iota(jnp.int32,(M,LEN),1)
        o,dq,g=pieces(stack(qd[:,:G]),stack(qd[:,G:]),[main+(vis,)],None)
        og[:,:G]=unstack(o); og[:,G:]=unstack(dq)
        add(off,g[0])
        for ref,d,first in ((g0,0,0),(g1,1,0),(g2,3,0),(g3,2,0),(g4,2,HALF)):
            n=ref.shape[0]; at=slab_at(x,d)+first
            ref[:,:HD]=(kg[:,pl.ds(at,n)]*SCALE).T.astype(H)
            ref[:,HD:]=vg[:,pl.ds(at,n)].T.astype(H)

G=GROUP*HD
def call(info,qa,da,qb,db,qd,slabs,ka,va,kb,vb):
    near=pl.BlockSpec((ROWS,G),lambda u,s:(jnp.minimum(u,3),s[4]))
    far=pl.BlockSpec((ROWS,G),lambda u,s:(jnp.clip(u-4,0,3),0))
    full=lambda *shape: pl.BlockSpec(shape,lambda u,s:(0,0))
    half=pl.BlockSpec((SLOTS,HD),lambda u,s:(0,s[4]))
    out=lambda *shape: jax.ShapeDtypeStruct(shape,H)
    whole=full(SLAB,2*HD); part=full(HALF,2*HD); own=full(SLOTS,2*HD)
    scratch=[(HD,2*LEN,F),(HD,2*LEN,F),(HD,SLOTS,F),(HD,SLOTS,F),(2*LEN,HD,H),(2*LEN,2*HD,H)]
    return pl.pallas_call(kernel,
        grid_spec=pltpu.PrefetchScalarGridSpec(num_scalar_prefetch=1,grid=(9,),
            in_specs=[near,near,far,far,full(ROWS,2*G)]+[whole]*4+[half,half]+[full(SLOTS,HD)]*2,
            out_specs=[near,near,far,far,full(ROWS,2*G)]+[whole]*3+[part]*2+[own]*2,
            scratch_shapes=[pltpu.VMEM(s[:2],s[2]) for s in scratch]),
        out_shape=[out(SLOTS,2*G),out(SLOTS,2*G),out(SLOTS,G),out(SLOTS,G),out(ROWS,2*G)]+[out(SLAB,2*HD)]*3+[out(HALF,2*HD)]*2+[out(SLOTS,2*HD)]*2,
        compiler_params=pltpu.CompilerParams(vmem_limit_bytes=56*1024*1024),
        name="attn")(info,qa,da,qb,db,qd,*slabs,ka,va,kb,vb)

def spread_kernel(k,v,out):
    for core in range(2):
        for head in range(4):
            cols=pl.ds((2*head+core)*HD,HD)
            piece=jnp.concatenate([k[:,cols],v[:,cols]],axis=1)
            for z in range(8): out[z*8+core*4+head]=piece

def spread(pk,pv):
    return pl.pallas_call(spread_kernel,out_shape=jax.ShapeDtypeStruct((64,8,2*HD),H),name="spread")(pk,pv)

ALL=("x","z","core","head")
PLANE=("z","core","head")
PAIR=("core","head")

def exchange(v,axes): return lax.all_to_all(v,axes,split_axis=0,concat_axis=0,tiled=True)
def swap(v): return lax.ppermute(v,"core",[(0,1),(1,0)])
def shift(v,d): return lax.ppermute(v,"x",[(i,(i+d)%4) for i in range(4)])
def by_head(v,width):
    return v.reshape(8,4,2,width).transpose(2,1,0,3).reshape(8,8,width)
def to_rows(v,width):
    return v.reshape(2,4,8,width).transpose(2,1,0,3).reshape(8,8*width)

def shards(pq,pk,pv,pd,rq,rk,rv,rd,parent,lengths):
    x=lax.axis_index("x"); z=lax.axis_index("z"); core=lax.axis_index("core")
    slab=exchange(spread(pk,pv),PLANE).reshape(SLAB,2*HD)
    slabs=(slab,shift(slab,1),shift(slab,3),shift(slab,2))
    other=1-core
    far=lambda v,w: swap(lax.dynamic_slice_in_dim(v,other*w,w,1))
    kb,vb=far(rk,HD),far(rv,HD)
    qb,db=far(rq,G),far(rd,G)
    theirs=swap(jnp.concatenate([parent,lengths]))
    qd=exchange(jnp.concatenate([by_head(pq,G),by_head(pd,G)],axis=2),PAIR).reshape(ROWS,2*G)
    row=(x*8+z)*ROWS
    prompt=row//LEN
    at=lax.broadcasted_iota(jnp.int32,(8,),0)
    info=jnp.zeros((8,),jnp.int32)
    for i,v in enumerate((parent[0],theirs[0],lengths[0],theirs[1],core,prompt,row-prompt*LEN,x)):
        info=jnp.where(at==i,v,info)
    oa,ga,ob,gb,og,g0,g1,g2,g3,g4,owna,ownb=call(info,rq,rd,qb,db,qd,slabs,rk,rv,kb,vb)
    g4=shift(shift(g4,3),3)
    opposite=jnp.concatenate([shift(g3,2),g4],axis=0)
    part=(g0.astype(F)+shift(g1,1).astype(F)+shift(g2,3).astype(F)+opposite.astype(F)).astype(H)
    ownb=swap(ownb)
    og,ownb=lax.optimization_barrier((og,ownb))
    back=exchange(og.reshape(8,8,2*G),PAIR)
    back,part=lax.optimization_barrier((back,part))
    tot=exchange(part.reshape(64,8,2*HD),PLANE).reshape(8,8,8,2*HD).astype(F).sum(0).astype(H)
    ob,gb=swap(ob),swap(gb)
    ro=lax.dynamic_update_slice_in_dim(oa,ob,other*G,1)
    rg=lax.dynamic_update_slice_in_dim(ga,gb,other*G,1)
    first=jnp.where(core==0,owna,ownb); second=jnp.where(core==0,ownb,owna)
    rkg=jnp.concatenate([first[:,:HD],second[:,:HD]],axis=1)
    rvg=jnp.concatenate([first[:,HD:],second[:,HD:]],axis=1)
    return (to_rows(back[:,:,:G],G),to_rows(back[:,:,G:],G),to_rows(tot[:,:,:HD],HD),to_rows(tot[:,:,HD:],HD),ro,rg,rkg,rvg)

def solution(mesh):
    fine=Mesh(mesh.devices.reshape(4,8,2,4),ALL)
    ctx=("x","z","core")
    rows=P(ALL,None); cols=P(ctx,"head")
    return jax.shard_map(shards,mesh=fine,in_specs=(rows,)*4+(cols,)*4+(P(ctx),)*2,out_specs=(rows,)*4+(cols,)*4,check_vma=False)
```
